32 devices in a mesh: groups: 2 (over y), lat: 4 (over z), lon: 2 (over x), section: 2 (over core).
Axes of the slice: x: 2, y: 2, z: 4, core: 2. Of those that a mesh axis runs over, the one named last changes fastest.
Arguments:
- features: bfloat16 [4, 200, 32, 256], P('groups', None, 'lat', 'lon'), parts along dimension 0, may hold values from -6 to 6
- ocean_tiles: int32 [4, 32], P('lat', 'lon'), may hold values 0 or 1
- kernels: float32 [2, 200, 49], P('section'), may hold values from -0.875 to 0.875
- norm_gains: float32 [2, 200], P('section'), may hold values from 0.5 to 2
- weights_in: bfloat16 [2, 200, 800], P('section'), may hold values from -0.4375 to 0.4375
- biases_in: float32 [2, 800], P('section'), may hold values from -3 to 3
- weights_out: bfloat16 [2, 800, 200], P('section'), may hold values from -0.21875 to 0.21875
Outputs:
- section_features: bfloat16 [2, 4, 200, 32, 256], P('section', 'groups', None, 'lat', 'lon'), parts along dimension 1
The draws below stay inside these ranges and needn't reach their ends.
There are 2 independent parts, one for each index of `groups`. The reference program is written for one: setup_inputs(seed, part) draws one part's arguments, and reference() takes and returns one part's arrays. A program takes and returns all parts, laid end to end along the dimension named above; an argument that names none is the same for every part. Nothing has to cross between parts.
Inputs may be any that keep to these rules, and one draw needn't show every extreme that they name: `ocean_tiles`: 1 marks a tile of 8 x 8 cells as ocean, 0 as land.
All inputs are finite; a program needn't handle non-finite values. No bound on the sum of `ocean_tiles` on one device may be relied on, other than what follows from the above.
Results may differ from the reference program's by a relative error of at most 0.018.
Values may be sent and summed in bfloat16 or wider, within the bound.
A program may use at most 64 MiB of HBM per device.

```python
import math
import jax
import jax.numpy as jnp
from jax import lax

CH = 200
HIDDEN_SIZE = 800
KSIZE = 7
TILE = 8
MICRO = 2
SECTIONS = 2
NJ = 32
NI = 256


def plant(drawn, rng, smallest, largest):
    shape = drawn.shape
    index_at = [jax.random.randint(jax.random.fold_in(rng, axis), (), 0, shape[axis]) for axis in range(len(shape))]
    drawn = drawn.at[tuple(index_at)].set(smallest)
    longest = shape.index(max(shape))
    index_at[longest] = (index_at[longest] + 1) % shape[longest]
    return drawn.at[tuple(index_at)].set(largest)


def level_of(key, shape, shards, smallest, largest):
    loudness, own = 1.0, jax.random.fold_in(key, 6)
    for axis_at, shards_of in shards:
        steps = jnp.exp(jax.random.uniform(jax.random.fold_in(own, axis_at), (shards_of,), jnp.float32, smallest / len(shards), largest / len(shards)))
        loudness = loudness * jnp.repeat(steps, shape[axis_at] // shards_of).reshape([-1 if axis == axis_at else 1 for axis in range(len(shape))])
    return loudness


def noise(stream_key, shape, width, most, cuts=(), kind=jnp.bfloat16):
    array = jax.random.normal(stream_key, shape, jnp.float32) * width
    if len(cuts) > 0:
        array = level_of(stream_key, shape, cuts, -0.22, 0.18) * array
    return jnp.clip(array, min=-most, max=most).astype(kind)


def setup_inputs(seed: int = 0, part: int = 0) -> dict:
    key_of = jax.random.split(jax.random.key(seed), 8)
    part_keys = jax.random.split(jax.random.fold_in(key_of[7], part), 8)
    features = noise(part_keys[0], (MICRO, CH, NJ, NI), 1.0, 6.0, ((2, 4), (3, 2)))
    ocean_tiles = plant((jax.random.randint(key_of[1], (NJ // TILE, NI // TILE), 0, 4) < 3).astype(jnp.int32), jax.random.fold_in(key_of[1], 1), 0, 1)
    kernels = noise(key_of[2], (SECTIONS, CH, KSIZE * KSIZE), (KSIZE * KSIZE) ** -0.5, 0.875, ((0, 2),), jnp.float32)
    norm_gains = jnp.clip(jnp.exp(math.log(2.0) - 1.3862944 * jax.random.uniform(key_of[3], (SECTIONS, CH), jnp.float32) ** level_of(key_of[3], (SECTIONS, CH), ((0, 2),), -0.2, 0.2)), 0.5, 2.0)
    weights_in = noise(key_of[4], (SECTIONS, CH, HIDDEN_SIZE), CH ** -0.5, 0.4375, ((0, 2),))
    biases_in = noise(key_of[5], (SECTIONS, HIDDEN_SIZE), 0.5, 3.0, ((0, 2),), jnp.float32)
    weights_out = noise(key_of[6], (SECTIONS, HIDDEN_SIZE, CH), HIDDEN_SIZE ** -0.5, 0.21875, ((0, 2),))
    return {"features": features, "ocean_tiles": ocean_tiles, "kernels": kernels, "norm_gains": norm_gains, "weights_in": weights_in, "biases_in": biases_in, "weights_out": weights_out}


def pad_field(field):
    reach = KSIZE // 2
    columns = jnp.concatenate([field[:, :, -reach:], field, field[:, :, :reach]], axis=2)
    north = columns[:, -reach:, :][:, ::-1, ::-1]
    south = jnp.zeros_like(north)
    return jnp.concatenate([south, columns, north], axis=1)

def depthwise(padded, kernel, rows, cols):
    total = jnp.zeros((padded.shape[0], rows, cols), jnp.float32)
    for row_shift in range(KSIZE):
        for col_shift in range(KSIZE):
            weight = kernel[:, row_shift * KSIZE + col_shift][:, None, None]
            window = padded[:, row_shift:row_shift + rows, col_shift:col_shift + cols].astype(jnp.float32)
            total = total + weight * window
    return total

def pointwise(normed_flat, weight_in, bias_in, weight_out):
    hidden = jnp.dot(weight_in.T, normed_flat, preferred_element_type=jnp.float32) + bias_in[:, None]
    active = jax.nn.gelu(hidden, approximate=False).astype(jnp.bfloat16)
    return jnp.dot(weight_out.T, active, preferred_element_type=jnp.float32)

def section_block(field, mask, kernel, gain, weight_in, bias_in, weight_out):
    mixed = depthwise(pad_field(field), kernel, NJ, NI)
    centre = lax.optimization_barrier(jnp.mean(mixed, axis=0, keepdims=True))
    centred = mixed - centre
    variance = lax.optimization_barrier(jnp.mean(centred * centred, axis=0, keepdims=True))
    normed = (centred * lax.rsqrt(variance + 1e-06) * gain[:, None, None]).astype(jnp.bfloat16)
    pieces = normed.reshape(CH, NJ // 8, 8 * NI).transpose(1, 0, 2)
    update = lax.map(lambda piece: pointwise(piece, weight_in, bias_in, weight_out), pieces)
    update = update.transpose(1, 0, 2).reshape(CH, NJ, NI)
    return (field.astype(jnp.float32) + mask * update).astype(jnp.bfloat16)

def reference(features, ocean_tiles, kernels, norm_gains, weights_in, biases_in, weights_out):
    mask = jnp.repeat(jnp.repeat(ocean_tiles, TILE, axis=0), TILE, axis=1).astype(jnp.float32)
    per_section = []
    currents = [features[micro_id] for micro_id in range(MICRO)]
    for section_id in range(SECTIONS):
        currents = [section_block(current, mask, kernels[section_id], norm_gains[section_id], weights_in[section_id], biases_in[section_id], weights_out[section_id]) for current in currents]
        per_section.append(jnp.stack(currents, axis=0))
    return jnp.stack(per_section, axis=0)
```

```python
import functools

import jax
import jax.numpy as jnp
from jax import lax
from jax.experimental import pallas as pl
from jax.experimental.pallas import tpu as pltpu
from jax.sharding import PartitionSpec as P

MESH = pl.DeviceIdType.MESH
KSIZE = 7
REACH = 3
TILE = 8
BLOCK = 16
BF = jnp.bfloat16
F32 = jnp.float32


def selection(shape, fn):
    r = lax.broadcasted_iota(jnp.int32, shape, 0)
    c = lax.broadcasted_iota(jnp.int32, shape, 1)
    return jnp.where(fn(r, c), 1.0, 0.0).astype(BF)


def dot(a, b):
    return jnp.dot(a, b, preferred_element_type=F32)


def kernel(n_lat, n_lon, ch, hid, rows, cols, chp,
           x_ref, tiles_ref, ker_ref, gain_ref, wi_ref, bias_ref, wo_ref, out_ref,
           ker_s, gain_s, wi_s, bias_s, wo_s, xp, hal, nb, pk, pw, pe, pc, pcn, pcs,
           kb, gb, wit, wot, mixed, nrm, act,
           loc_sem, wsend, wrecv, psend, precv, rsend, rrecv, csend, crecv, osend, orecv):
    lat = lax.axis_index("lat")
    lon = lax.axis_index("lon")
    sec = lax.axis_index("section")
    other = 1 - sec
    is_top = lat == n_lat - 1
    has_south = lat > 0
    north_lat = jnp.where(is_top, lat, lat + 1)
    north_lon = jnp.where(is_top, n_lon - 1 - lon, lon)
    south_lat = jnp.where(has_south, lat - 1, lat)
    east = lax.rem(lon + 1, n_lon)
    west = lax.rem(lon + n_lon - 1, n_lon)
    partner = {"section": other}
    north = {"lat": north_lat, "lon": north_lon}
    south = {"lat": south_lat}
    sides = [({"lon": west}, pe, 1)] if n_lon == 2 else [({"lon": west}, pe, 1), ({"lon": east}, pw, 0)]

    load = pltpu.make_async_copy(x_ref, xp.at[0, pl.ds(REACH, rows)], loc_sem.at[5])
    load.start()
    barrier = pltpu.get_barrier_semaphore()
    pl.semaphore_signal(barrier, inc=1, device_id=partner, device_id_type=MESH)
    pl.semaphore_signal(barrier, inc=1, device_id=north, device_id_type=MESH)
    for device, _, _ in sides:
        pl.semaphore_signal(barrier, inc=1, device_id=device, device_id_type=MESH)

    @pl.when(has_south)
    def _():
        pl.semaphore_signal(barrier, inc=1, device_id=south, device_id_type=MESH)

    @pl.when(lat == 0)
    def _():
        for s in range(2):
            xp[s, 0:REACH] = jnp.zeros((REACH, chp, cols), BF)
            pcs[s] = jnp.zeros((chp, cols), BF)

    pl.semaphore_wait(barrier, 2 + len(sides) + jnp.where(has_south, 1, 0))

    params = [(ker_ref, ker_s), (gain_ref, gain_s), (bias_ref, bias_s), (wi_ref, wi_s), (wo_ref, wo_s)]
    sent = []
    for k, (src, dst) in enumerate(params):
        copy = pltpu.make_async_remote_copy(
            src_ref=src, dst_ref=dst.at[sec], send_sem=wsend.at[k], recv_sem=wrecv.at[k],
            device_id=partner, device_id_type=MESH)
        copy.start()
        own = pltpu.make_async_copy(src, dst.at[sec], loc_sem.at[k])
        own.start()
        sent.append((copy, own))

    lane_slot = selection((cols, cols), lambda r, c: r == cols - 1 - c)
    ident = selection((cols, cols), lambda r, c: r == c)
    turn = jnp.where(is_top, lane_slot.astype(F32), ident.astype(F32)).astype(BF)

    def halo_matrix(j):
        return selection((cols, cols), lambda r, c: ((c < REACH) & (r == 16 * j + c)) | (
            (c >= cols - REACH) & (r == 16 * j + 8 + c - (cols - REACH))))

    def pack_matrix(j):
        return selection((cols, cols), lambda r, c: ((r < REACH) & (c == 16 * j + r)) | (
            (r >= cols - REACH) & (c == 16 * j + 8 + r - (cols - REACH))))

    def start_pack(s):
        total = jnp.zeros((chp, cols), F32)
        for j in range(rows):
            total = total + dot(xp[s, REACH + j], pack_matrix(j))
        pk[s] = total.astype(BF)
        copies = []
        for k, (device, dst, _) in enumerate(sides):
            copy = pltpu.make_async_remote_copy(
                src_ref=pk.at[s], dst_ref=dst.at[s], send_sem=psend.at[s, k], recv_sem=precv.at[s, k],
                device_id=device, device_id_type=MESH)
            copy.start()
            copies.append(copy)
        return copies

    def rows_north(s):
        return (
            pltpu.make_async_remote_copy(
                src_ref=xp.at[s, pl.ds(rows, REACH)], dst_ref=xp.at[s, pl.ds(0, REACH)],
                send_sem=rsend.at[s, 0], recv_sem=rrecv.at[s, 0], device_id=north, device_id_type=MESH),
            pltpu.make_async_remote_copy(
                src_ref=xp.at[s, pl.ds(rows, REACH)], dst_ref=nb.at[s],
                send_sem=rsend.at[s, 0], recv_sem=rrecv.at[s, 1], device_id=north, device_id_type=MESH),
        )

    def rows_south(s):
        return pltpu.make_async_remote_copy(
            src_ref=xp.at[s, pl.ds(REACH, REACH)], dst_ref=nb.at[s],
            send_sem=rsend.at[s, 1], recv_sem=rrecv.at[s, 1], device_id=south, device_id_type=MESH)

    def packs_north(s):
        return (
            pltpu.make_async_remote_copy(
                src_ref=pc.at[s], dst_ref=pcs.at[s],
                send_sem=csend.at[s, 0], recv_sem=crecv.at[s, 0], device_id=north, device_id_type=MESH),
            pltpu.make_async_remote_copy(
                src_ref=pc.at[s], dst_ref=pcn.at[s],
                send_sem=csend.at[s, 0], recv_sem=crecv.at[s, 1], device_id=north, device_id_type=MESH),
        )

    def packs_south(s):
        return pltpu.make_async_remote_copy(
            src_ref=pc.at[s], dst_ref=pcn.at[s],
            send_sem=csend.at[s, 1], recv_sem=crecv.at[s, 1], device_id=south, device_id_type=MESH)

    def start_both(to_north, to_south):
        @pl.when(is_top)
        def _():
            to_north[1].start()

        @pl.when(jnp.logical_not(is_top))
        def _():
            to_north[0].start()

        @pl.when(has_south)
        def _():
            to_south.start()

    def wait_recv_both(to_north):
        to_north[1].wait_recv()

        @pl.when(has_south)
        def _():
            to_north[0].wait_recv()

    def wait_send_both(to_north, to_south):
        to_north[0].wait_send()

        @pl.when(has_south)
        def _():
            to_south.wait_send()

    def prepare_conv(s):
        gain = gain_s[s]
        diag = lax.broadcasted_iota(jnp.int32, (ch, ch), 0) == lax.broadcasted_iota(jnp.int32, (ch, ch), 1)
        column = jnp.sum(jnp.where(diag, jnp.broadcast_to(gain, (ch, ch)), 0.0), axis=1, keepdims=True)
        gb[s] = jnp.broadcast_to(column, (ch, cols))
        taps = ker_s[s]
        taps = jnp.concatenate([taps, jnp.zeros((chp - ch, taps.shape[1]), F32)], axis=0).astype(BF)

        def one(t, carry):
            r = lax.broadcasted_iota(jnp.int32, (KSIZE * KSIZE, cols), 0)
            spread = jnp.where(r == t, 1.0, 0.0).astype(BF)
            kb[s, t] = dot(taps, spread).astype(BF)
            return carry

        lax.fori_loop(0, KSIZE * KSIZE, one, 0)

    def prepare_weights(s):
        b = bias_s[s]
        hi = b.astype(BF).astype(F32)
        mid = (b - hi).astype(BF).astype(F32)
        low = (b - hi - mid).astype(BF).astype(F32)
        tail = jnp.concatenate([hi, mid, low, jnp.zeros((chp - ch - 3, hid), F32)], axis=0)
        whole = jnp.concatenate([wi_s[s].astype(F32), tail], axis=0)
        wit[s] = whole.T.astype(BF)
        wot[s] = (wo_s[s].astype(F32) * 0.5).T.astype(BF)

    tail_row = lax.broadcasted_iota(jnp.int32, (chp - ch, cols), 0)
    ones_tail = jnp.where(tail_row < 3, 1.0, 0.0).astype(F32)
    tile_cols = tiles_ref.shape[1]
    spread = selection((tile_cols, cols), lambda r, c: c // TILE == r)
    mask = dot(jnp.broadcast_to(tiles_ref[...].astype(F32).astype(BF), (8, tile_cols)), spread)[0:1]
    mask2 = jnp.concatenate([mask, mask], axis=1)

    def wait_params(k):
        sent[k][1].wait()
        sent[k][0].wait()

    load.wait()
    sends_out = []
    for s in range(2):
        to_north, to_south = rows_north(s), rows_south(s)
        start_both(to_north, to_south)
        pack_copies = start_pack(s)
        if s == 0:
            wait_params(0)
            wait_params(1)
            prepare_conv(0)
        for copy in pack_copies:
            copy.wait_recv()
        if n_lon == 2:
            pc[s] = pe[s]
        else:
            lane = lax.broadcasted_iota(jnp.int32, (chp, cols), 1)
            pc[s] = jnp.where(lax.rem(lane, 16) < 8, pe[s].astype(F32), pw[s].astype(F32)).astype(BF)
        pnorth, psouth = packs_north(s), packs_south(s)
        start_both(pnorth, psouth)

        def own_halo(j, carry):
            hal[REACH + j] = dot(pc[s], halo_matrix(j)).astype(BF)
            return carry

        lax.fori_loop(0, rows, own_halo, 0)
        if s == 0:
            wait_params(2)
            wait_params(3)
            wait_params(4)
            prepare_conv(1)
            prepare_weights(0)
            prepare_weights(1)
        wait_recv_both(to_north)
        wait_recv_both(pnorth)
        for k in range(REACH):
            row = jnp.where(is_top, REACH - 1 - k, k)
            xp[s, REACH + rows + k] = dot(nb[s, row], turn).astype(BF)
            j = jnp.where(is_top, rows - 1 - k, k)
            hal[REACH + rows + k] = dot(dot(pcn[s], halo_matrix(j)).astype(BF), turn).astype(BF)
            hal[k] = dot(pcs[s], halo_matrix(rows - REACH + k)).astype(BF)

        def conv(t, carry):
            at = pl.ds(pl.multiple_of(t * BLOCK, BLOCK), BLOCK)
            lane = lax.broadcasted_iota(jnp.int32, (BLOCK, cols), 1)
            acc = [None] * rows
            for b in range(KSIZE):
                d = b - REACH
                shifted = []
                for r in range(rows + 2 * REACH):
                    x = xp[s, r, at, :]
                    if d != 0:
                        h = hal[r, at, :]
                        x = jnp.where(lane < d if d > 0 else lane >= cols + d, h, x)
                        x = pltpu.roll(x, (-d) % cols, 1)
                    shifted.append(x)
                weights = [kb[s, a * KSIZE + b, at, :] for a in range(KSIZE)]
                for j in range(rows):
                    part = weights[0] * shifted[j]
                    for a in range(1, KSIZE):
                        part = part + weights[a] * shifted[j + a]
                    part = part.astype(F32)
                    acc[j] = part if acc[j] is None else acc[j] + part
            for j in range(rows):
                mixed[j, at, :] = acc[j]
            return carry

        lax.fori_loop(0, chp // BLOCK, conv, 0)

        def point(i, carry):
            for k in range(2):
                m = mixed[2 * i + k, 0:ch, :]
                centre = jnp.sum(m, axis=0, keepdims=True) * (1.0 / ch)
                m = m - centre
                var = jnp.sum(m * m, axis=0, keepdims=True) * (1.0 / ch)
                m = m * lax.rsqrt(var + 1e-6) * gb[s]
                nrm[:, k * cols:(k + 1) * cols] = jnp.concatenate([m, ones_tail], axis=0).astype(BF)
            chunk = 160
            for q in range(hid // chunk):
                h = dot(wit[s, q * chunk:(q + 1) * chunk], nrm[...])
                act[q * chunk:(q + 1) * chunk] = (h * (1.0 + lax.erf(h * 0.7071067811865476))).astype(BF)
            update = dot(wot[s], act[...]) * mask2
            for k in range(2):
                row = REACH + 2 * i + k
                x = xp[s, row, 0:ch, :].astype(F32) + update[:, k * cols:(k + 1) * cols]
                xp[s + 1, row] = jnp.concatenate([x, jnp.zeros((chp - ch, cols), F32)], axis=0).astype(BF)
            return carry

        lax.fori_loop(0, rows // 2, point, 0)
        result = xp.at[s + 1, pl.ds(REACH, rows)]
        here = pltpu.make_async_copy(result, out_ref.at[sec], osend.at[s])
        there = pltpu.make_async_remote_copy(
            src_ref=result, dst_ref=out_ref.at[sec], send_sem=osend.at[s], recv_sem=orecv.at[0],
            device_id=partner, device_id_type=MESH)

        @pl.when(sec == s)
        def _():
            here.start()

        @pl.when(sec != s)
        def _():
            there.start()

        sends_out.append((here, there))
        for copy in pack_copies:
            copy.wait_send()
        wait_send_both(to_north, to_south)
        wait_send_both(pnorth, psouth)

    for s in range(2):
        here, there = sends_out[s]

        @pl.when(sec == s)
        def _():
            here.wait()

        @pl.when(sec != s)
        def _():
            there.wait_send()

    sends_out[0][1].wait_recv()


def on_device(features, ocean_tiles, kernels, norm_gains, weights_in, biases_in, weights_out):
    n_lat, n_lon = lax.axis_size("lat"), lax.axis_size("lon")
    micro, ch, rows, cols = features.shape
    hid = weights_in.shape[2]
    chp = -(-ch // BLOCK) * BLOCK
    padded = rows + 2 * REACH
    state = lax.dynamic_index_in_dim(features, lax.axis_index("section"), 0, keepdims=False)
    state = jnp.pad(state.transpose(1, 0, 2), ((0, 0), (0, chp - ch), (0, 0)))
    any_spec = pl.BlockSpec(memory_space=pl.ANY)
    vmem = pl.BlockSpec(memory_space=pltpu.VMEM)
    V = pltpu.VMEM
    dma = pltpu.SemaphoreType.DMA
    pack = (2, chp, cols)
    out = pl.pallas_call(
        functools.partial(kernel, n_lat, n_lon, ch, hid, rows, cols, chp),
        out_shape=jax.ShapeDtypeStruct((micro, rows, chp, cols), BF),
        in_specs=[any_spec, vmem] + [any_spec] * 5,
        out_specs=any_spec,
        scratch_shapes=[
            V((2, ch, KSIZE * KSIZE), F32), V((2, 1, ch), F32), V((2, ch, hid), BF), V((2, 1, hid), F32),
            V((2, hid, ch), BF),
            V((3, padded, chp, cols), BF), V((padded, chp, cols), BF), V((2, REACH, chp, cols), BF),
            V(pack, BF), V(pack, BF), V(pack, BF), V(pack, BF), V(pack, BF), V(pack, BF),
            V((2, KSIZE * KSIZE, chp, cols), BF), V((2, ch, cols), F32), V((2, hid, chp), BF), V((2, ch, hid), BF),
            V((rows, chp, cols), F32), V((chp, 2 * cols), BF), V((hid, 2 * cols), BF),
            dma((6,)), dma((5,)), dma((5,)), dma((2, 2)), dma((2, 2)), dma((2, 2)), dma((2, 2)),
            dma((2, 2)), dma((2, 2)), dma((2,)), dma((1,)),
        ],
        compiler_params=pltpu.CompilerParams(
            collective_id=0, has_side_effects=True, vmem_limit_bytes=40 * 1024 * 1024),
    )(state, ocean_tiles, kernels[0], norm_gains, weights_in[0], biases_in, weights_out[0])
    return out[:, :, :ch, :].transpose(0, 2, 1, 3)[None]


def solution(mesh):
    return jax.shard_map(
        on_device,
        mesh=mesh,
        in_specs=(
            P("groups", None, "lat", "lon"),
            P("lat", "lon"),
            P("section", None, None),
            P("section", None),
            P("section", None, None),
            P("section", None),
            P("section", None, None),
        ),
        out_specs=P("section", "groups", None, "lat", "lon"),
        check_vma=False,
    )
```

```python
import functools

import jax
import jax.numpy as jnp
from jax import lax
from jax.experimental import pallas as pl
from jax.experimental.pallas import tpu as pltpu
from jax.sharding import PartitionSpec as P

MESH = pl.DeviceIdType.MESH
KSIZE = 7
REACH = 3
TILE = 8
BLOCK = 16
BF = jnp.bfloat16
F32 = jnp.float32


def selection(shape, fn):
    r = lax.broadcasted_iota(jnp.int32, shape, 0)
    c = lax.broadcasted_iota(jnp.int32, shape, 1)
    return jnp.where(fn(r, c), 1.0, 0.0).astype(BF)


def dot(a, b):
    return jnp.dot(a, b, preferred_element_type=F32)


def kernel(n_lat, n_lon, ch, hid, rows, cols, chp,
           x_ref, tiles_ref, ker_ref, gain_ref, wi_ref, bias_ref, wo_ref, out_ref,
           ker_s, gain_s, wi_s, bias_s, wo_s, xp, hal, nb, pk, pw, pe, pc, pcn, pcs, zz,
           smat, umat, utn, kb, gb, wit, wot, mixed, nrm, act,
           loc_sem, wsend, wrecv, psend, precv, rsend, rrecv, csend, crecv, osend, orecv):
    lat = lax.axis_index("lat")
    lon = lax.axis_index("lon")
    sec = lax.axis_index("section")
    is_top = lat == n_lat - 1
    has_south = lat > 0
    partner = {"section": 1 - sec}
    north = {"lat": jnp.where(is_top, lat, lat + 1), "lon": jnp.where(is_top, n_lon - 1 - lon, lon)}
    south = {"lat": jnp.where(has_south, lat - 1, lat)}
    east = lax.rem(lon + 1, n_lon)
    west = lax.rem(lon + n_lon - 1, n_lon)
    sides = [({"lon": west}, pe)] if n_lon == 2 else [({"lon": west}, pe), ({"lon": east}, pw)]
    pairs = rows // 2
    tiles = chp // BLOCK

    load = pltpu.make_async_copy(x_ref, xp.at[0, pl.ds(REACH, rows)], loc_sem.at[5])
    load.start()
    barrier = pltpu.get_barrier_semaphore()
    pl.semaphore_signal(barrier, inc=1, device_id=partner, device_id_type=MESH)
    pl.semaphore_signal(barrier, inc=1, device_id=north, device_id_type=MESH)
    for device, _ in sides:
        pl.semaphore_signal(barrier, inc=1, device_id=device, device_id_type=MESH)

    @pl.when(has_south)
    def _():
        pl.semaphore_signal(barrier, inc=1, device_id=south, device_id_type=MESH)

    @pl.when(lat == 0)
    def _():
        for s in range(2):
            xp[s, 0:REACH] = jnp.zeros((REACH, chp, cols), BF)
            pcs[s] = jnp.zeros((2, 2 * BLOCK, cols), BF)

    smat[...] = selection((2 * cols, cols), lambda r, c: (
        ((r % cols < REACH) & (c % 16 == (r // cols) * 8 + r % cols))
        | ((r % cols >= cols - REACH) & (c % 16 == (r // cols) * 8 + 4 + r % cols - (cols - REACH)))))
    flip = selection((cols, cols), lambda r, c: r == cols - 1 - c).astype(F32)
    ident = selection((cols, cols), lambda r, c: r == c).astype(F32)
    turn = jnp.where(is_top, flip, ident).astype(BF)
    for q in range(2):
        unit = selection((cols, cols), lambda r, c: (
            ((c < REACH) & (r == 8 * q + c)) | ((c >= cols - REACH) & (r == 8 * q + 4 + c - (cols - REACH)))))
        umat[q] = unit
        utn[q] = dot(unit, turn).astype(BF)

    def pack(s, i):
        both = jnp.concatenate([xp[s, REACH + 2 * i], xp[s, REACH + 2 * i + 1]], axis=1)
        spread = dot(both, smat[...])
        group = lax.broadcasted_iota(jnp.int32, (BLOCK, cols), 1) // 16
        for h in range(2):
            total = jnp.zeros((BLOCK, cols), F32)
            for t in range(8 * h, min(8 * h + 8, tiles)):
                total = jnp.where(group == t % 8, spread[t * BLOCK:(t + 1) * BLOCK], total)
            pk[s, i, h * BLOCK:(h + 1) * BLOCK] = total.astype(BF)

    def pack_copies(s, i):
        return [pltpu.make_async_remote_copy(
            src_ref=pk.at[s, i], dst_ref=dst.at[s, i], send_sem=psend.at[s, i, k], recv_sem=precv.at[s, i, k],
            device_id=device, device_id_type=MESH) for k, (device, dst) in enumerate(sides)]

    def remote(src, dst, send, recv, device):
        return pltpu.make_async_remote_copy(
            src_ref=src, dst_ref=dst, send_sem=send, recv_sem=recv, device_id=device, device_id_type=MESH)

    def rows_north(s, part):
        at, into, fold, size = ((rows + 1, 1, 1, 2), (rows, 0, 0, 1))[part]
        block = xp.at[s, pl.ds(at, size)]
        send = rsend.at[s, 0, part]
        return (remote(block, xp.at[s, pl.ds(into, size)], send, rrecv.at[s, 0, part], north),
                remote(block, nb.at[s, pl.ds(fold, size)], send, rrecv.at[s, 1, part], north))

    def rows_south(s, part):
        at, into, size = ((REACH, 0, 2), (REACH + 2, 2, 1))[part]
        return remote(xp.at[s, pl.ds(at, size)], nb.at[s, pl.ds(into, size)],
                      rsend.at[s, 1, part], rrecv.at[s, 1, part], south)

    def packs_north(s):
        block = pc.at[s, pl.ds(pairs - 2, 2)]
        return (remote(block, pcs.at[s], csend.at[s, 0], crecv.at[s, 0], north),
                remote(block, pcn.at[s], csend.at[s, 0], crecv.at[s, 1], north))

    def packs_south(s):
        return remote(pc.at[s, pl.ds(0, 2)], pcn.at[s], csend.at[s, 1], crecv.at[s, 1], south)

    def start_north(copies):
        @pl.when(is_top)
        def _():
            copies[1].start()

        @pl.when(jnp.logical_not(is_top))
        def _():
            copies[0].start()

    def if_south(act_on):
        @pl.when(has_south)
        def _():
            act_on()

    def combine(s, i):
        for copy in pack_copies(s, i):
            copy.wait_recv()
        if n_lon == 2:
            pc[s, i] = pe[s, i]
        else:
            lane = lax.broadcasted_iota(jnp.int32, (2 * BLOCK, cols), 1)
            pc[s, i] = jnp.where(lane % 8 < 4, pe[s, i].astype(F32), pw[s, i].astype(F32)).astype(BF)

    def unpack(packed):
        for t in range(tiles):
            part = packed[(t // 8) * BLOCK:(t // 8 + 1) * BLOCK]
            zz[t * BLOCK:(t + 1) * BLOCK] = pltpu.roll(part, (-16 * (t % 8)) % cols, 1) if t % 8 else part
        return zz[...]

    def prepare_conv(s):
        gain = gain_s[s]
        diag = lax.broadcasted_iota(jnp.int32, (ch, ch), 0) == lax.broadcasted_iota(jnp.int32, (ch, ch), 1)
        column = jnp.sum(jnp.where(diag, jnp.broadcast_to(gain, (ch, ch)), 0.0), axis=1, keepdims=True)
        gb[s] = jnp.broadcast_to(column, (ch, cols))
        taps = ker_s[s].T
        for t in range(KSIZE * KSIZE):
            kb[s, t, 0:ch] = jnp.broadcast_to(taps[:, t:t + 1], (ch, cols))
            kb[s, t, ch:chp] = jnp.zeros((chp - ch, cols), F32)

    def prepare_weights(s):
        b = bias_s[s]
        hi = b.astype(BF).astype(F32)
        mid = (b - hi).astype(BF).astype(F32)
        low = (b - hi - mid).astype(BF).astype(F32)
        tail = jnp.concatenate([hi, mid, low, jnp.zeros((chp - ch - 3, hid), F32)], axis=0)
        whole = jnp.concatenate([wi_s[s].astype(F32), tail], axis=0)
        wit[s] = whole.T.astype(BF)
        wot[s] = (wo_s[s].astype(F32) * 0.5).astype(BF)

    tail_row = lax.broadcasted_iota(jnp.int32, (chp - ch, cols), 0)
    ones_tail = jnp.where(tail_row < 3, 1.0, 0.0).astype(F32)
    tile_cols = tiles_ref.shape[1]
    spread_tiles = selection((tile_cols, cols), lambda r, c: c // TILE == r)
    mask = dot(jnp.broadcast_to(tiles_ref[...].astype(F32).astype(BF), (8, tile_cols)), spread_tiles)[0:1]
    mask2 = jnp.concatenate([mask, mask], axis=1)

    load.wait()
    for i in range(pairs):
        pack(0, i)
    pl.semaphore_wait(barrier, 2 + len(sides) + jnp.where(has_south, 1, 0))

    params = [(ker_ref, ker_s), (gain_ref, gain_s), (bias_ref, bias_s), (wi_ref, wi_s), (wo_ref, wo_s)]
    moved = []
    for i in range(pairs):
        for copy in pack_copies(0, i):
            copy.start()
    for k, (src, dst) in enumerate(params):
        copy = remote(src, dst.at[sec], wsend.at[k], wrecv.at[k], partner)
        copy.start()
        own = pltpu.make_async_copy(src, dst.at[sec], loc_sem.at[k])
        own.start()
        moved.append((copy, own))
        if k == 1:
            for part in range(2):
                start_north(rows_north(0, part))
                if_south(rows_south(0, part).start)

    def wait_params(k):
        moved[k][1].wait()
        moved[k][0].wait()

    def shift(x, h, d, lane):
        if d == 0:
            return x.astype(F32)
        x = jnp.where(lane < d if d > 0 else lane >= cols + d, h, x)
        return pltpu.roll(x, (-d) % cols, 1).astype(F32)

    def conv_pass(s, sources, first):
        def body(t, carry):
            at = pl.ds(pl.multiple_of(t * BLOCK, BLOCK), BLOCK)
            lane = lax.broadcasted_iota(jnp.int32, (BLOCK, cols), 1)
            acc = {}
            for b in range(KSIZE):
                d = b - REACH
                shifted = {r: shift(xp[s, r, at, :], hal[r, at, :] if d else None, d, lane) for r in sources}
                for a in range(KSIZE):
                    used = [j for j in range(rows) if j + a in shifted]
                    if not used:
                        continue
                    weight = kb[s, a * KSIZE + b, at, :]
                    for j in used:
                        term = weight * shifted[j + a]
                        acc[j] = acc[j] + term if j in acc else term
            for j in acc:
                mixed[j, at, :] = acc[j] if first else mixed[j, at, :] + acc[j]
            return carry

        lax.fori_loop(0, tiles, body, 0)

    def out_copies(s, i):
        block = xp.at[s + 1, pl.ds(REACH + 2 * i, 2)]
        into = out_ref.at[sec, pl.ds(2 * i, 2)]
        return (pltpu.make_async_copy(block, into, osend.at[s, i]),
                remote(block, into, osend.at[s, i], orecv.at[i], partner))

    def point(s, i):
        for k in range(2):
            m = mixed[2 * i + k, 0:ch, :]
            centre = jnp.sum(m, axis=0, keepdims=True) * (1.0 / ch)
            m = m - centre
            var = jnp.sum(m * m, axis=0, keepdims=True) * (1.0 / ch)
            m = m * lax.rsqrt(var + 1e-6) * gb[s]
            nrm[:, k * cols:(k + 1) * cols] = jnp.concatenate([m, ones_tail], axis=0).astype(BF)
        chunk = 160
        for q in range(hid // chunk):
            h = dot(wit[s, q * chunk:(q + 1) * chunk], nrm[...])
            act[q * chunk:(q + 1) * chunk] = (h * (1.0 + lax.erf(h * 0.7071067811865476))).astype(BF)
        update = dot(wot[s], act[...]) * mask2
        for k in range(2):
            row = REACH + 2 * i + k
            x = xp[s, row, 0:ch, :].astype(F32) + update[:, k * cols:(k + 1) * cols]
            xp[s + 1, row] = jnp.concatenate([x, jnp.zeros((chp - ch, cols), F32)], axis=0).astype(BF)
        here, there = out_copies(s, i)

        @pl.when(sec == s)
        def _():
            here.start()

        @pl.when(sec != s)
        def _():
            there.start()

    for s in range(2):
        if s == 0:
            wait_params(0)
            wait_params(1)
            prepare_conv(0)
        for i in range(pairs - 1, pairs - 3, -1):
            combine(s, i)
        start_north(packs_north(s))
        if s == 1:
            prepare_conv(1)
        for i in range(2):
            combine(s, i)
        if_south(packs_south(s).start)
        for i in range(pairs):
            held = unpack(pc[s, i])
            for q in range(2):
                hal[REACH + 2 * i + q] = dot(held, umat[q]).astype(BF)
        conv_pass(s, range(REACH, REACH + rows), True)
        if s == 0:
            for k in range(2, 5):
                wait_params(k)
            prepare_weights(0)
            prepare_weights(1)
        for part in range(2):
            rows_north(s, part)[1].wait_recv()
            if_south(rows_north(s, part)[0].wait_recv)
        packs_north(s)[1].wait_recv()
        if_south(packs_north(s)[0].wait_recv)
        for k in range(REACH):
            row = jnp.where(is_top, REACH - 1 - k, k)
            xp[s, REACH + rows + k] = dot(nb[s, row], turn).astype(BF)
        for p in range(2):
            held = unpack(pcn[s, jnp.where(is_top, 1 - p, p)])
            for q in range(2):
                k = 2 * p + q
                if k < REACH:
                    hal[REACH + rows + k] = dot(held, utn[jnp.where(is_top, 1 - q, q)]).astype(BF)
            held = unpack(pcs[s, p])
            for q in range(2):
                k = 2 * p + q - 1
                if k >= 0:
                    hal[k] = dot(held, umat[q]).astype(BF)
        conv_pass(s, [*range(REACH), *range(REACH + rows, 2 * REACH + rows)], False)
        for i in (pairs - 1, 0, pairs - 2, 1):
            point(s, i)
            if s == 0:
                part = 0 if i in (0, pairs - 1) else 1
                if i >= pairs - 2:
                    start_north(rows_north(1, part))
                else:
                    if_south(rows_south(1, part).start)
                pack(1, i)
                for copy in pack_copies(1, i):
                    copy.start()

    for s in range(2):
        for i in range(pairs):
            here, there = out_copies(s, i)

            @pl.when(sec == s)
            def _():
                here.wait()

            @pl.when(sec != s)
            def _():
                there.wait_send()

            for copy in pack_copies(s, i):
                copy.wait_send()
        for part in range(2):
            rows_north(s, part)[0].wait_send()
            if_south(rows_south(s, part).wait_send)
        packs_north(s)[0].wait_send()
        if_south(packs_south(s).wait_send)
    for i in range(pairs):
        out_copies(0, i)[1].wait_recv()


def on_device(features, ocean_tiles, kernels, norm_gains, weights_in, biases_in, weights_out):
    n_lat, n_lon = lax.axis_size("lat"), lax.axis_size("lon")
    micro, ch, rows, cols = features.shape
    hid = weights_in.shape[2]
    chp = -(-ch // BLOCK) * BLOCK
    padded = rows + 2 * REACH
    state = lax.dynamic_index_in_dim(features, lax.axis_index("section"), 0, keepdims=False)
    state = jnp.pad(state.transpose(1, 0, 2), ((0, 0), (0, chp - ch), (0, 0)))
    any_spec = pl.BlockSpec(memory_space=pl.ANY)
    vmem = pl.BlockSpec(memory_space=pltpu.VMEM)
    V = pltpu.VMEM
    dma = pltpu.SemaphoreType.DMA
    pairs = rows // 2
    pack = (2, pairs, 2 * BLOCK, cols)
    edge = (2, 2, 2 * BLOCK, cols)
    hbm = pl.BlockSpec(memory_space=pltpu.HBM)
    out = pl.pallas_call(
        functools.partial(kernel, n_lat, n_lon, ch, hid, rows, cols, chp),
        out_shape=jax.ShapeDtypeStruct((micro, rows, chp, cols), BF),
        in_specs=[any_spec, vmem] + [hbm] * 5,
        out_specs=any_spec,
        scratch_shapes=[
            V((2, KSIZE * KSIZE, ch), F32), V((2, 1, ch), F32), V((2, ch, hid), BF), V((2, 1, hid), F32),
            V((2, ch, hid), BF),
            V((3, padded, chp, cols), BF), V((padded, chp, cols), BF), V((2, REACH, chp, cols), BF),
            V(pack, BF), V(pack, BF), V(pack, BF), V(pack, BF), V(edge, BF), V(edge, BF), V((chp, cols), BF),
            V((2 * cols, cols), BF), V((2, cols, cols), BF), V((2, cols, cols), BF),
            V((2, KSIZE * KSIZE, chp, cols), F32), V((2, ch, cols), F32), V((2, hid, chp), BF), V((2, ch, hid), BF),
            V((rows, chp, cols), F32), V((chp, 2 * cols), BF), V((hid, 2 * cols), BF),
            dma((6,)), dma((5,)), dma((5,)), dma((2, pairs, 2)), dma((2, pairs, 2)), dma((2, 2, 2)), dma((2, 2, 2)),
            dma((2, 2)), dma((2, 2)), dma((2, pairs)), dma((pairs,)),
        ],
        compiler_params=pltpu.CompilerParams(
            collective_id=0, has_side_effects=True, vmem_limit_bytes=40 * 1024 * 1024),
    )(state, ocean_tiles, kernels[0].T, norm_gains, weights_in[0], biases_in, weights_out[0].T)
    return out[:, :, :ch, :].transpose(0, 2, 1, 3)[None]


def solution(mesh):
    return jax.shard_map(
        on_device,
        mesh=mesh,
        in_specs=(
            P("groups", None, "lat", "lon"),
            P("lat", "lon"),
            P("section", None, None),
            P("section", None),
            P("section", None, None),
            P("section", None),
            P("section", None, None),
        ),
        out_specs=P("section", "groups", None, "lat", "lon"),
        check_vma=False,
    )
```

```python
import functools

import jax
import jax.numpy as jnp
from jax import lax
from jax.experimental import pallas as pl
from jax.experimental.pallas import tpu as pltpu
from jax.sharding import PartitionSpec as P

MESH = pl.DeviceIdType.MESH
KSIZE = 7
REACH = 3
TILE = 8
BLOCK = 16
BF = jnp.bfloat16
F32 = jnp.float32


def selection(shape, fn):
    r = lax.broadcasted_iota(jnp.int32, shape, 0)
    c = lax.broadcasted_iota(jnp.int32, shape, 1)
    return jnp.where(fn(r, c), 1.0, 0.0).astype(BF)


def dot(a, b):
    return jnp.dot(a, b, preferred_element_type=F32)


def kernel(n_lat, n_lon, ch, hid, rows, cols, chp,
           x_ref, tiles_ref, ker_ref, gain_ref, wi_ref, bias_ref, wo_ref, out_ref,
           ker_s, gain_s, wi_s, bias_s, wo_s, xp, hal, nb, pk, pw, pe, pc, pcn, pcs, zz,
           smat, umat, utn, kb, gb, wit, wot, mixed, nrm, act,
           loc_sem, wsend, wrecv, psend, precv, rsend, rrecv, csend, crecv, osend, orecv):
    lat = lax.axis_index("lat")
    lon = lax.axis_index("lon")
    sec = lax.axis_index("section")
    is_top = lat == n_lat - 1
    has_south = lat > 0
    partner = {"section": 1 - sec}
    north = {"lat": jnp.where(is_top, lat, lat + 1), "lon": jnp.where(is_top, n_lon - 1 - lon, lon)}
    south = {"lat": jnp.where(has_south, lat - 1, lat)}
    east = lax.rem(lon + 1, n_lon)
    west = lax.rem(lon + n_lon - 1, n_lon)
    sides = [({"lon": west}, pe)] if n_lon == 2 else [({"lon": west}, pe), ({"lon": east}, pw)]
    pairs = rows // 2
    tiles = chp // BLOCK

    load = pltpu.make_async_copy(x_ref, xp.at[0, pl.ds(REACH, rows)], loc_sem.at[5])
    load.start()
    barrier = pltpu.get_barrier_semaphore()
    pl.semaphore_signal(barrier, inc=1, device_id=partner, device_id_type=MESH)
    pl.semaphore_signal(barrier, inc=1, device_id=north, device_id_type=MESH)
    for device, _ in sides:
        pl.semaphore_signal(barrier, inc=1, device_id=device, device_id_type=MESH)

    @pl.when(has_south)
    def _():
        pl.semaphore_signal(barrier, inc=1, device_id=south, device_id_type=MESH)

    @pl.when(lat == 0)
    def _():
        for s in range(2):
            xp[s, 0:REACH] = jnp.zeros((REACH, chp, cols), BF)
            pcs[s] = jnp.zeros((2, 2 * BLOCK, cols), BF)

    smat[...] = selection((2 * cols, cols), lambda r, c: (
        ((r % cols < REACH) & (c % 16 == (r // cols) * 8 + r % cols))
        | ((r % cols >= cols - REACH) & (c % 16 == (r // cols) * 8 + 4 + r % cols - (cols - REACH)))))
    flip = selection((cols, cols), lambda r, c: r == cols - 1 - c).astype(F32)
    ident = selection((cols, cols), lambda r, c: r == c).astype(F32)
    turn = jnp.where(is_top, flip, ident).astype(BF)
    for q in range(2):
        unit = selection((cols, cols), lambda r, c: (
            ((c < REACH) & (r == 8 * q + c)) | ((c >= cols - REACH) & (r == 8 * q + 4 + c - (cols - REACH)))))
        umat[q] = unit
        utn[q] = dot(unit, turn).astype(BF)

    def pack(s, i):
        both = jnp.concatenate([xp[s, REACH + 2 * i], xp[s, REACH + 2 * i + 1]], axis=1)
        spread = dot(both, smat[...])
        group = lax.broadcasted_iota(jnp.int32, (BLOCK, cols), 1) // 16
        for h in range(2):
            total = jnp.zeros((BLOCK, cols), F32)
            for t in range(8 * h, min(8 * h + 8, tiles)):
                total = jnp.where(group == t % 8, spread[t * BLOCK:(t + 1) * BLOCK], total)
            pk[s, i, h * BLOCK:(h + 1) * BLOCK] = total.astype(BF)

    def pack_copies(s, i):
        return [pltpu.make_async_remote_copy(
            src_ref=pk.at[s, i], dst_ref=dst.at[s, i], send_sem=psend.at[s, i, k], recv_sem=precv.at[s, i, k],
            device_id=device, device_id_type=MESH) for k, (device, dst) in enumerate(sides)]

    def remote(src, dst, send, recv, device):
        return pltpu.make_async_remote_copy(
            src_ref=src, dst_ref=dst, send_sem=send, recv_sem=recv, device_id=device, device_id_type=MESH)

    def rows_north(s, part):
        at, into, fold, size = ((rows + 1, 1, 1, 2), (rows, 0, 0, 1))[part]
        block = xp.at[s, pl.ds(at, size)]
        send = rsend.at[s, 0, part]
        return (remote(block, xp.at[s, pl.ds(into, size)], send, rrecv.at[s, 0, part], north),
                remote(block, nb.at[s, pl.ds(fold, size)], send, rrecv.at[s, 1, part], north))

    def rows_south(s, part):
        at, into, size = ((REACH, 0, 2), (REACH + 2, 2, 1))[part]
        return remote(xp.at[s, pl.ds(at, size)], nb.at[s, pl.ds(into, size)],
                      rsend.at[s, 1, part], rrecv.at[s, 1, part], south)

    def packs_north(s):
        block = pc.at[s, pl.ds(pairs - 2, 2)]
        return (remote(block, pcs.at[s], csend.at[s, 0], crecv.at[s, 0], north),
                remote(block, pcn.at[s], csend.at[s, 0], crecv.at[s, 1], north))

    def packs_south(s):
        return remote(pc.at[s, pl.ds(0, 2)], pcn.at[s], csend.at[s, 1], crecv.at[s, 1], south)

    def start_north(copies):
        @pl.when(is_top)
        def _():
            copies[1].start()

        @pl.when(jnp.logical_not(is_top))
        def _():
            copies[0].start()

    def if_south(act_on):
        @pl.when(has_south)
        def _():
            act_on()

    def combine(s, i):
        for copy in pack_copies(s, i):
            copy.wait_recv()
        if n_lon == 2:
            pc[s, i] = pe[s, i]
        else:
            lane = lax.broadcasted_iota(jnp.int32, (2 * BLOCK, cols), 1)
            pc[s, i] = jnp.where(lane % 8 < 4, pe[s, i].astype(F32), pw[s, i].astype(F32)).astype(BF)

    def unpack(packed):
        for t in range(tiles):
            part = packed[(t // 8) * BLOCK:(t // 8 + 1) * BLOCK]
            zz[t * BLOCK:(t + 1) * BLOCK] = pltpu.roll(part, (-16 * (t % 8)) % cols, 1) if t % 8 else part
        return zz[...]

    def prepare_conv(s):
        gain = gain_s[s]
        diag = lax.broadcasted_iota(jnp.int32, (ch, ch), 0) == lax.broadcasted_iota(jnp.int32, (ch, ch), 1)
        column = jnp.sum(jnp.where(diag, jnp.broadcast_to(gain, (ch, ch)), 0.0), axis=1, keepdims=True)
        gb[s] = jnp.broadcast_to(column, (ch, cols))
        taps = ker_s[s, :, 0, :].T
        for t in range(KSIZE * KSIZE):
            kb[s, t, 0:ch] = jnp.broadcast_to(taps[:, t:t + 1], (ch, cols))
            kb[s, t, ch:chp] = jnp.zeros((chp - ch, cols), F32)

    def prepare_weights(s):
        b = bias_s[s]
        hi = b.astype(BF).astype(F32)
        mid = (b - hi).astype(BF).astype(F32)
        low = (b - hi - mid).astype(BF).astype(F32)
        tail = jnp.concatenate([hi, mid, low, jnp.zeros((chp - ch - 3, hid), F32)], axis=0)
        whole = jnp.concatenate([wi_s[s].astype(F32), tail], axis=0)
        wit[s] = whole.T.astype(BF)
        wot[s] = (wo_s[s].astype(F32) * 0.5).astype(BF)

    tail_row = lax.broadcasted_iota(jnp.int32, (chp - ch, cols), 0)
    ones_tail = jnp.where(tail_row < 3, 1.0, 0.0).astype(F32)
    tile_cols = tiles_ref.shape[1]
    spread_tiles = selection((tile_cols, cols), lambda r, c: c // TILE == r)
    mask = dot(jnp.broadcast_to(tiles_ref[...].astype(F32).astype(BF), (8, tile_cols)), spread_tiles)[0:1]
    mask2 = jnp.concatenate([mask, mask], axis=1)

    load.wait()
    for i in range(pairs):
        pack(0, i)
    pl.semaphore_wait(barrier, 2 + len(sides) + jnp.where(has_south, 1, 0))

    params = [(ker_ref, ker_s), (gain_ref, gain_s), (bias_ref, bias_s), (wi_ref, wi_s), (wo_ref, wo_s)]
    moved = []
    for i in range(pairs):
        for copy in pack_copies(0, i):
            copy.start()
    for k, (src, dst) in enumerate(params):
        copy = remote(src, dst.at[sec], wsend.at[k], wrecv.at[k], partner)
        copy.start()
        own = pltpu.make_async_copy(src, dst.at[sec], loc_sem.at[k])
        own.start()
        moved.append((copy, own))
        if k == 1:
            for part in range(2):
                start_north(rows_north(0, part))
                if_south(rows_south(0, part).start)

    def wait_params(k):
        moved[k][1].wait()
        moved[k][0].wait()

    def shift(x, h, d, lane):
        if d == 0:
            return x.astype(F32)
        x = jnp.where(lane < d if d > 0 else lane >= cols + d, h, x)
        return pltpu.roll(x, (-d) % cols, 1).astype(F32)

    def conv_pass(s, sources, first):
        def body(t, carry):
            at = pl.ds(pl.multiple_of(t * BLOCK, BLOCK), BLOCK)
            lane = lax.broadcasted_iota(jnp.int32, (BLOCK, cols), 1)
            acc = {}
            for b in range(KSIZE):
                d = b - REACH
                shifted = {r: shift(xp[s, r, at, :], hal[r, at, :] if d else None, d, lane) for r in sources}
                for a in range(KSIZE):
                    used = [j for j in range(rows) if j + a in shifted]
                    if not used:
                        continue
                    weight = kb[s, a * KSIZE + b, at, :]
                    for j in used:
                        term = weight * shifted[j + a]
                        acc[j] = acc[j] + term if j in acc else term
            for j in acc:
                mixed[j, at, :] = acc[j] if first else mixed[j, at, :] + acc[j]
            return carry

        lax.fori_loop(0, tiles, body, 0, unroll=not first)

    def out_copies(s, i):
        block = xp.at[s + 1, pl.ds(REACH + 2 * i, 2)]
        into = out_ref.at[sec, pl.ds(2 * i, 2)]
        return (pltpu.make_async_copy(block, into, osend.at[s, i]),
                remote(block, into, osend.at[s, i], orecv.at[i], partner))

    def point(s, i):
        for k in range(2):
            m = mixed[2 * i + k, 0:ch, :]
            centre = jnp.sum(m, axis=0, keepdims=True) * (1.0 / ch)
            m = m - centre
            var = jnp.sum(m * m, axis=0, keepdims=True) * (1.0 / ch)
            m = m * lax.rsqrt(var + 1e-6) * gb[s]
            nrm[:, k * cols:(k + 1) * cols] = jnp.concatenate([m, ones_tail], axis=0).astype(BF)
        chunk = 160
        for q in range(hid // chunk):
            h = dot(wit[s, q * chunk:(q + 1) * chunk], nrm[...])
            act[q * chunk:(q + 1) * chunk] = (h * (1.0 + lax.erf(h * 0.7071067811865476))).astype(BF)
        update = dot(wot[s], act[...]) * mask2
        for k in range(2):
            row = REACH + 2 * i + k
            x = xp[s, row, 0:ch, :].astype(F32) + update[:, k * cols:(k + 1) * cols]
            xp[s + 1, row] = jnp.concatenate([x, jnp.zeros((chp - ch, cols), F32)], axis=0).astype(BF)
        here, there = out_copies(s, i)

        @pl.when(sec == s)
        def _():
            here.start()

        @pl.when(sec != s)
        def _():
            there.start()

    for s in range(2):
        if s == 0:
            wait_params(0)
            wait_params(1)
            prepare_conv(0)
        for i in range(pairs - 1, pairs - 3, -1):
            combine(s, i)
        start_north(packs_north(s))
        if s == 1:
            prepare_conv(1)
        for i in range(2):
            combine(s, i)
        if_south(packs_south(s).start)
        for i in range(pairs):
            held = unpack(pc[s, i])
            for q in range(2):
                hal[REACH + 2 * i + q] = dot(held, umat[q]).astype(BF)
        conv_pass(s, range(REACH, REACH + rows), True)
        if s == 0:
            for k in range(2, 5):
                wait_params(k)
            prepare_weights(0)
            prepare_weights(1)
        for part in range(2):
            rows_north(s, part)[1].wait_recv()
            if_south(rows_north(s, part)[0].wait_recv)
        packs_north(s)[1].wait_recv()
        if_south(packs_north(s)[0].wait_recv)
        for k in range(REACH):
            row = jnp.where(is_top, REACH - 1 - k, k)
            xp[s, REACH + rows + k] = dot(nb[s, row], turn).astype(BF)
        for p in range(2):
            held = unpack(pcn[s, jnp.where(is_top, 1 - p, p)])
            for q in range(2):
                k = 2 * p + q
                if k < REACH:
                    hal[REACH + rows + k] = dot(held, utn[jnp.where(is_top, 1 - q, q)]).astype(BF)
            held = unpack(pcs[s, p])
            for q in range(2):
                k = 2 * p + q - 1
                if k >= 0:
                    hal[k] = dot(held, umat[q]).astype(BF)
        conv_pass(s, [*range(REACH), *range(REACH + rows, 2 * REACH + rows)], False)
        for i in (pairs - 1, 0, pairs - 2, 1):
            point(s, i)
            if s == 0:
                part = 0 if i in (0, pairs - 1) else 1
                if i >= pairs - 2:
                    start_north(rows_north(1, part))
                else:
                    if_south(rows_south(1, part).start)
                pack(1, i)
                for copy in pack_copies(1, i):
                    copy.start()

    for s in range(2):
        for i in range(pairs):
            here, there = out_copies(s, i)

            @pl.when(sec == s)
            def _():
                here.wait()

            @pl.when(sec != s)
            def _():
                there.wait_send()

            for copy in pack_copies(s, i):
                copy.wait_send()
        for part in range(2):
            rows_north(s, part)[0].wait_send()
            if_south(rows_south(s, part).wait_send)
        packs_north(s)[0].wait_send()
        if_south(packs_south(s).wait_send)
    for i in range(pairs):
        out_copies(0, i)[1].wait_recv()


def on_device(features, ocean_tiles, kernels, norm_gains, weights_in, biases_in, weights_out):
    n_lat, n_lon = lax.axis_size("lat"), lax.axis_size("lon")
    micro, ch, rows, cols = features.shape
    hid = weights_in.shape[2]
    chp = -(-ch // BLOCK) * BLOCK
    padded = rows + 2 * REACH
    state = lax.dynamic_index_in_dim(features, lax.axis_index("section"), 0, keepdims=False)
    state = jnp.pad(state.transpose(1, 0, 2), ((0, 0), (0, chp - ch), (0, 0)))
    any_spec = pl.BlockSpec(memory_space=pl.ANY)
    vmem = pl.BlockSpec(memory_space=pltpu.VMEM)
    V = pltpu.VMEM
    dma = pltpu.SemaphoreType.DMA
    pairs = rows // 2
    pack = (2, pairs, 2 * BLOCK, cols)
    edge = (2, 2, 2 * BLOCK, cols)
    hbm = pl.BlockSpec(memory_space=pltpu.HBM)
    out = pl.pallas_call(
        functools.partial(kernel, n_lat, n_lon, ch, hid, rows, cols, chp),
        out_shape=jax.ShapeDtypeStruct((micro, rows, chp, cols), BF),
        in_specs=[any_spec, vmem] + [hbm] * 5,
        out_specs=any_spec,
        scratch_shapes=[
            V((2, KSIZE * KSIZE, 1, ch), F32), V((2, 1, ch), F32), V((2, ch, hid), BF), V((2, 1, hid), F32),
            V((2, ch, hid), BF),
            V((3, padded, chp, cols), BF), V((padded, chp, cols), BF), V((2, REACH, chp, cols), BF),
            V(pack, BF), V(pack, BF), V(pack, BF), V(pack, BF), V(edge, BF), V(edge, BF), V((chp, cols), BF),
            V((2 * cols, cols), BF), V((2, cols, cols), BF), V((2, cols, cols), BF),
            V((2, KSIZE * KSIZE, chp, cols), F32), V((2, ch, cols), F32), V((2, hid, chp), BF), V((2, ch, hid), BF),
            V((rows, chp, cols), F32), V((chp, 2 * cols), BF), V((hid, 2 * cols), BF),
            dma((6,)), dma((5,)), dma((5,)), dma((2, pairs, 2)), dma((2, pairs, 2)), dma((2, 2, 2)), dma((2, 2, 2)),
            dma((2, 2)), dma((2, 2)), dma((2, pairs)), dma((pairs,)),
        ],
        compiler_params=pltpu.CompilerParams(
            collective_id=0, has_side_effects=True, vmem_limit_bytes=40 * 1024 * 1024),
    )(state, ocean_tiles, kernels.transpose(2, 0, 1), norm_gains, weights_in[0], biases_in, weights_out[0].T)
    return out[:, :, :ch, :].transpose(0, 2, 1, 3)[None]


def solution(mesh):
    return jax.shard_map(
        on_device,
        mesh=mesh,
        in_specs=(
            P("groups", None, "lat", "lon"),
            P("lat", "lon"),
            P("section", None, None),
            P("section", None),
            P("section", None, None),
            P("section", None),
            P("section", None, None),
        ),
        out_specs=P("section", "groups", None, "lat", "lon"),
        check_vma=False,
    )
```
